32 devices in a mesh: img: 2 (over y), space: 16 (over z, x, core).
Axes of the slice: x: 2, y: 2, z: 4, core: 2. Of those that a mesh axis runs over, the one named last changes fastest.
Arguments:
- images: float32 [2, 384, 96, 128], P('img', 'space'), may hold values from -6 to 6
- pairings: int32 [3, 2], replicated, may hold values from 0 to 1, as said below
Outputs:
- advected: float32 [2, 384, 96, 128], P('img', 'space')
- velocity: float32 [2, 3, 384, 96, 128], P('img', None, 'space')
The draws below stay inside these ranges and needn't reach their ends.
Inputs may be any that keep to these rules, and one draw needn't show every extreme that they name: Each row of pairings is a permutation of the 2 images; an image may be its own partner.
All inputs are finite; a program needn't handle non-finite values.
Results may differ from the reference program's by a relative error of at most 0.00018.
Values sent between devices are 32-bit elements; how exact they have to be, the bound alone decides.
No kernel may reach another device: no remote copies, remote signals or barrier semaphores. Data moves between devices by JAX's collectives and lax.ppermute only.
A program may use at most 64 MiB of HBM per device.

```python
import math
import jax
import jax.numpy as jnp
from jax import lax

Y = 96
Z = 128
RADIUS = 4
PAIRINGS = 3
IMAGES = 2
NX = 384


def draw_pairings(key, part):
    row_list = []
    for row_number in range(PAIRINGS):
        shuffled = jax.random.permutation(jax.random.fold_in(key, 17 + row_number), IMAGES).astype(jnp.int32)
        row_list.append(shuffled)
    return jnp.stack(row_list).astype(jnp.int32)


def levels(rng, dims, pieces, smallest, largest):
    loudness, own = 1.0, jax.random.fold_in(rng, 6)
    for axis_at, shards_of in pieces:
        heights = jnp.exp(jax.random.uniform(jax.random.fold_in(own, axis_at), (shards_of,), jnp.float32, smallest / len(pieces), largest / len(pieces)))
        loudness = loudness * jnp.repeat(heights, dims[axis_at] // shards_of).reshape([-1 if axis == axis_at else 1 for axis in range(len(dims))])
    return loudness


def bell_draw(rng, extent, scale, most, pieces=(), kind=jnp.bfloat16):
    values = jax.random.normal(rng, extent, jnp.float32) * scale
    if len(pieces) > 0:
        values = levels(rng, extent, pieces, -0.22, 0.18) * values
    return jnp.clip(values, min=-most, max=most).astype(kind)


def setup_inputs(seed: int = 0) -> dict:
    keys = jax.random.split(jax.random.key(seed), 3)
    return {
        "images": bell_draw(keys[0], (IMAGES, NX, Y, Z), 1.0, 6.0, ((0, 2), (1, 16)), jnp.float32),
        "pairings": draw_pairings(jax.random.fold_in(keys[2], 71), 0),
    }


gauss_sigma = 1.5
step_scale = 8.0
floor_product = 0.25
floor_variance = 0.5


def gauss_taps(radius):
    raw_taps = [math.exp(-(offset * offset) / (2.0 * gauss_sigma * gauss_sigma)) for offset in range(-radius, radius + 1)]
    total_weight = sum(raw_taps)
    return [raw_weight / total_weight for raw_weight in raw_taps]


def padded_along(volume, dimension, margin):
    widths = [(0, 0)] * volume.ndim
    widths[dimension] = (margin, margin)
    return jnp.pad(volume, widths)


def window(padded, dimension, offset, length):
    return lax.slice_in_dim(padded, offset, offset + length, axis=dimension)


def sum_three(volume, dimension):
    length = volume.shape[dimension]
    padded = padded_along(volume, dimension, 1)
    return window(padded, dimension, 0, length) + window(padded, dimension, 1, length) + window(padded, dimension, 2, length)


def box_mean(volume):
    return sum_three(sum_three(volume, 0), 1) / 9.0


def central(volume, dimension):
    length = volume.shape[dimension]
    padded = padded_along(volume, dimension, 1)
    return (window(padded, dimension, 2, length) - window(padded, dimension, 0, length)) * 0.5


def smooth_along(volume, dimension, weights):
    length = volume.shape[dimension]
    padded = padded_along(volume, dimension, len(weights) // 2)
    result = weights[0] * window(padded, dimension, 0, length)
    for tap_index in range(1, len(weights)):
        result = result + weights[tap_index] * window(padded, dimension, tap_index, length)
    return result


def advect(volume, velocity):
    change = None
    for dimension in range(3):
        length = volume.shape[dimension]
        padded = padded_along(volume, dimension, 1)
        backward = volume - window(padded, dimension, 0, length)
        forward = window(padded, dimension, 2, length) - volume
        speed_part = velocity[dimension]
        part_change = jnp.maximum(speed_part, 0.0) * backward + jnp.minimum(speed_part, 0.0) * forward
        change = part_change if change is None else change + part_change
    return volume - change


def correlation_drive(own_brick, partner):
    mean_own = box_mean(own_brick)
    mean_partner = box_mean(partner)
    cross_term = box_mean(own_brick * partner) - mean_own * mean_partner
    spread_own = box_mean(own_brick * own_brick) - mean_own * mean_own
    spread_partner = box_mean(partner * partner) - mean_partner * mean_partner
    factor = 2.0 * cross_term / jnp.maximum(spread_own * spread_partner, floor_product)
    ratio_term = cross_term / jnp.maximum(spread_own, floor_variance)
    return factor * ((partner - mean_partner) - ratio_term * (own_brick - mean_own))


def reference(images, pairings):
    weights = gauss_taps(RADIUS)

    def one_image(image_index):
        own_brick = lax.dynamic_index_in_dim(images, image_index, 0, keepdims=False)
        drive_sum = None
        for pairing_row in range(PAIRINGS):
            partner_index = lax.dynamic_index_in_dim(pairings[pairing_row], image_index, 0, keepdims=False)
            partner = lax.dynamic_index_in_dim(images, partner_index, 0, keepdims=False)
            pair_term = correlation_drive(own_brick, partner)
            drive_sum = pair_term if drive_sum is None else drive_sum + pair_term
        gradient = jnp.stack([central(own_brick, 0), central(own_brick, 1), central(own_brick, 2)])
        force = drive_sum[None] * gradient
        smoothed = smooth_along(force, 1, weights)
        smoothed = smooth_along(smoothed, 2, weights)
        smoothed = smooth_along(smoothed, 3, weights)
        velocity = step_scale * smoothed
        return advect(own_brick, velocity), velocity

    advected, velocity = lax.map(one_image, jnp.arange(IMAGES, dtype=jnp.int32))
    return advected, velocity
```

```python
import functools
import math

import jax
import jax.numpy as jnp
from jax import lax
from jax.experimental import pallas as pl
from jax.experimental.pallas import tpu as pltpu
from jax.sharding import PartitionSpec as P

RADIUS = 4
PAIRINGS = 3
HALO = RADIUS + 1
TILE = 8

gauss_sigma = 1.5
step_scale = 8.0
floor_product = 0.25
floor_variance = 0.5

CUTS = (0, 12)


def gauss_taps(radius):
    raw_taps = [
        math.exp(-(offset * offset) / (2.0 * gauss_sigma * gauss_sigma))
        for offset in range(-radius, radius + 1)
    ]
    total_weight = sum(raw_taps)
    return [raw_weight / total_weight for raw_weight in raw_taps]


WEIGHTS = gauss_taps(RADIUS)


def convolve(values, weights):
    half = len(weights) // 2
    result = weights[half] * values[half]
    for t in range(1, half + 1):
        result = result + weights[half + t] * (values[half - t] + values[half + t])
    return result


def band_matrix(width):
    row = lax.broadcasted_iota(jnp.int32, (width, width), 0)
    column = lax.broadcasted_iota(jnp.int32, (width, width), 1)
    away = jnp.abs(row - column)
    band = jnp.zeros((width, width), jnp.float32)
    for t in range(RADIUS + 1):
        band = jnp.where(away == t, WEIGHTS[RADIUS + t], band)
    high = band.astype(jnp.bfloat16)
    low = (band - high.astype(jnp.float32)).astype(jnp.bfloat16)
    above = jnp.concatenate([high, low], axis=1)
    below = jnp.concatenate([high, jnp.zeros_like(low)], axis=1)
    return jnp.concatenate([above, below], axis=0)


class Strip:
    def __init__(self, first, last, tiles, rows, width, partners):
        self.first, self.last, self.tiles = first, last, tiles
        self.rows, self.width, self.partners = rows, width, partners
        self.count = last - first
        self.low = max(first - 1, 0)
        self.high = min(last + 1, tiles)
        self.at_low, self.at_high = first == 0, last == tiles

    def local(self, tile):
        return tile - self.first + 1


def strip_kernel(strip, cuts, aliased, *refs):
    rows, width, partners = strip.rows, strip.width, strip.partners
    count = strip.count
    pieces = len(cuts)
    scalars, image, own_up, own_down, edge, far_up, far_down = refs[:7]
    middles = refs[7 : 7 + pieces]
    refs = refs[7 + pieces :]
    if aliased:
        refs = refs[2:]
    advected_out, velocity_out, a_buf, b_buf, d_buf, f_buf, v_buf, o_buf, in_sem, out_sem = refs

    def place(tile):
        return TILE * (strip.local(tile) + 1)

    span = TILE * (strip.high - strip.low)
    source = pl.ds(TILE * strip.low, span)
    target = pl.ds(place(strip.low), span)
    copies = []

    def fetch(src, dst):
        copy = pltpu.make_async_copy(src, dst, in_sem)
        copy.start()
        copies.append(copy)

    fetch(image.at[0, :, source, :], a_buf.at[pl.ds(HALO, rows), target, :])
    fetch(own_up.at[:, source, :], a_buf.at[pl.ds(0, HALO), target, :])
    fetch(own_down.at[:, source, :], a_buf.at[pl.ds(HALO + rows, HALO), target, :])
    for k in range(partners):
        fetch(edge.at[k, pl.ds(0, HALO), source, :], b_buf.at[k, pl.ds(HALO, HALO), target, :])
        fetch(edge.at[k, pl.ds(HALO, HALO), source, :], b_buf.at[k, pl.ds(rows, HALO), target, :])
        fetch(far_up.at[k, :, source, :], b_buf.at[k, pl.ds(0, HALO), target, :])
        fetch(far_down.at[k, :, source, :], b_buf.at[k, pl.ds(HALO + rows, HALO), target, :])
        for (begin, end), middle in zip(cuts, middles):
            low, high = max(begin, strip.low), min(end, strip.high)
            size = TILE * (high - low)
            fetch(
                middle.at[k, :, pl.ds(TILE * (low - begin), size), :],
                b_buf.at[k, pl.ds(2 * HALO, rows - 2 * HALO), pl.ds(place(low), size), :],
            )

    zero_tile = jnp.zeros((TILE, width), jnp.float32)
    for edge_here, tile in ((strip.at_low, 0), (strip.at_high, count + 1)):
        if edge_here:
            for i in range(rows + 2 * HALO):
                a_buf[i, pl.ds(TILE * (tile + 1), TILE), :] = zero_tile
                for k in range(partners):
                    b_buf[k, i, pl.ds(TILE * (tile + 1), TILE), :] = zero_tile
            for c in range(3):
                for r in range(rows):
                    f_buf[c, r, pl.ds(TILE * tile, TILE), :] = zero_tile

    bands = band_matrix(width)
    lane = lax.broadcasted_iota(jnp.int32, (TILE, width), 1)
    first_lane, last_lane = lane == 0, lane == width - 1

    def z_before(v):
        return jnp.where(first_lane, 0.0, pltpu.roll(v, 1, 1))

    def z_after(v):
        return jnp.where(last_lane, 0.0, pltpu.roll(v, width - 1, 1))

    for copy in copies:
        copy.wait()

    begin_tile = 1 if strip.at_low else 0
    end_tile = count + 1 if strip.at_high else count + 2
    drive_rows = rows + 2 * RADIUS
    ninth = 1.0 / 9.0

    self_weight = scalars[2]
    pair_weights = [scalars[3 + k] for k in range(partners)]

    def drive_tile(tile, carry):
        base = TILE * (tile + 1)

        def y_sums(i):
            def around(ref, *index):
                return [ref[(*index, pl.ds(base + s, TILE), slice(None))] for s in (-1, 0, 1)]

            def total(parts):
                return parts[0] + parts[1] + parts[2]

            a = around(a_buf, i)
            sums = [total(a), total([v * v for v in a])]
            centers = [a[1]]
            for k in range(partners):
                b = around(b_buf, k, i)
                sums += [total(b), total([v * v for v in b]), total([p * q for p, q in zip(a, b)])]
                centers.append(b[1])
            return sums, centers

        def finish(j, sums, centers):
            valid = scalars[0] if j < RADIUS else scalars[1] if j >= RADIUS + rows else None
            a = centers[0]
            mean_a = sums[0] * ninth
            spread_a = sums[1] * ninth - mean_a * mean_a
            guarded = jnp.maximum(spread_a, floor_variance)
            center_a = a - mean_a
            own = (2.0 * self_weight / floor_product) * spread_a
            own = own * jnp.maximum(1.0 - spread_a * (1.0 / floor_variance), 0.0)
            result = own * center_a
            for k in range(partners):
                sum_b, sum_bb, sum_ab = sums[2 + 3 * k : 5 + 3 * k]
                mean_b = sum_b * ninth
                cross = sum_ab * ninth - mean_a * mean_b
                spread_b = sum_bb * ninth - mean_b * mean_b
                product = jnp.maximum(spread_a * spread_b, floor_product)
                rest = (centers[1 + k] - mean_b) * guarded - cross * center_a
                result = result + (2.0 * pair_weights[k]) * cross * rest / (product * guarded)
            if valid is not None:
                result = result * valid
            d_buf[j, pl.ds(pl.multiple_of(TILE * tile, TILE), TILE), :] = result

        window = [y_sums(0), y_sums(1)]
        for j in range(0, drive_rows, 2):
            window += [y_sums(j + 2), y_sums(j + 3)]
            shared = [p + q for p, q in zip(window[1][0], window[2][0])]
            finish(j, [p + q for p, q in zip(window[0][0], shared)], window[1][1])
            finish(j + 1, [p + q for p, q in zip(shared, window[3][0])], window[2][1])
            window = window[2:]
        return carry

    lax.fori_loop(begin_tile, end_tile, drive_tile, 0)

    scaled = [w * (0.5 * step_scale) for w in WEIGHTS]

    def force_tile(tile, carry):
        base = TILE * (tile + 1)
        here = pl.ds(pl.multiple_of(TILE * tile, TILE), TILE)
        forces = ([], [], [])
        for j in range(drive_rows):
            drive = d_buf[j, here, :]
            a = a_buf[j + 1, pl.ds(base, TILE), :]
            forces[0].append(
                drive * (a_buf[j + 2, pl.ds(base, TILE), :] - a_buf[j, pl.ds(base, TILE), :])
            )
            forces[1].append(
                drive
                * (a_buf[j + 1, pl.ds(base + 1, TILE), :] - a_buf[j + 1, pl.ds(base - 1, TILE), :])
            )
            forces[2].append(drive * (z_after(a) - z_before(a)))
            r = j - 2 * RADIUS
            if r >= 0:
                for c in range(3):
                    f_buf[c, r, here, :] = convolve(forces[c][r : r + 2 * RADIUS + 1], scaled)
        return carry

    lax.fori_loop(begin_tile, end_tile, force_tile, 0)

    def finish_row(r, carry):
        smooth = []
        for c in range(3):
            for tile in range(1, count + 1):
                taps = [
                    f_buf[c, r, pl.ds(TILE * tile + s, TILE), :] for s in range(-RADIUS, RADIUS + 1)
                ]
                smooth.append(convolve(taps, WEIGHTS))
        smooth = jnp.concatenate(smooth, axis=0)
        high = smooth.astype(jnp.bfloat16)
        low = (smooth - high.astype(jnp.float32)).astype(jnp.bfloat16)
        both = jnp.dot(
            jnp.concatenate([high, low], axis=1), bands, preferred_element_type=jnp.float32
        )
        velocity = both[:, :width] + both[:, width:]
        for tile in range(1, count + 1):
            base = TILE * (tile + 1)
            i = r + HALO
            a = a_buf[i, pl.ds(base, TILE), :]
            neighbours = (
                (a_buf[i - 1, pl.ds(base, TILE), :], a_buf[i + 1, pl.ds(base, TILE), :]),
                (a_buf[i, pl.ds(base - 1, TILE), :], a_buf[i, pl.ds(base + 1, TILE), :]),
                (z_before(a), z_after(a)),
            )
            change = None
            there = pl.ds(TILE * (tile - 1), TILE)
            for c, (before, after) in enumerate(neighbours):
                at = TILE * (count * c + tile - 1)
                v = velocity[at : at + TILE]
                v_buf[c, r, there, :] = v
                part = v * jnp.where(v > 0.0, a - before, after - a)
                change = part if change is None else change + part
            o_buf[r, there, :] = a - change
        return carry

    there = pl.ds(TILE * strip.first, TILE * count)
    groups = 3
    each = rows // groups
    copies = []
    for g in range(groups):
        lax.fori_loop(g * each, (g + 1) * each, finish_row, 0)
        some = pl.ds(g * each, each)
        for src, dst in (
            (o_buf.at[some], advected_out.at[0, some, there, :]),
            (v_buf.at[:, some], velocity_out.at[0, :, some, there, :]),
        ):
            copy = pltpu.make_async_copy(src, dst, out_sem)
            copy.start()
            copies.append(copy)
    for copy in copies:
        copy.wait()


def run_strip(first, last, scalars, images, own_halos, edge, far_halos, middles, cuts, previous):
    _, rows, height, width = images.shape
    partners = edge.shape[0]
    strip = Strip(first, last, height // TILE, rows, width, partners)
    used = [
        (cut, middle)
        for cut, middle in zip(cuts, middles)
        if cut[0] < strip.high and cut[1] > strip.low
    ]
    operands = [scalars, images, *own_halos, edge, *far_halos, *(m for _, m in used)]
    in_specs = [pl.BlockSpec(memory_space=pltpu.SMEM)]
    in_specs += [pl.BlockSpec(memory_space=pl.ANY)] * (len(operands) - 1)
    aliases = {}
    if previous is not None:
        aliases = {len(operands): 0, len(operands) + 1: 1}
        operands += list(previous)
        in_specs += [pl.BlockSpec(memory_space=pl.ANY)] * 2
    extended, count = rows + 2 * HALO, strip.count
    f32 = jnp.float32
    voxels = rows * count * TILE * width
    return pl.pallas_call(
        functools.partial(
            strip_kernel, strip, [cut for cut, _ in used], previous is not None
        ),
        out_shape=(
            jax.ShapeDtypeStruct((1, rows, height, width), f32),
            jax.ShapeDtypeStruct((1, 3, rows, height, width), f32),
        ),
        in_specs=in_specs,
        out_specs=(pl.BlockSpec(memory_space=pl.ANY),) * 2,
        scratch_shapes=[
            pltpu.VMEM((extended, TILE * (count + 4), width), f32),
            pltpu.VMEM((partners, extended, TILE * (count + 4), width), f32),
            pltpu.VMEM((rows + 2 * RADIUS, TILE * (count + 2), width), f32),
            pltpu.VMEM((3, rows, TILE * (count + 2), width), f32),
            pltpu.VMEM((3, rows, TILE * count, width), f32),
            pltpu.VMEM((rows, TILE * count, width), f32),
            pltpu.SemaphoreType.DMA,
            pltpu.SemaphoreType.DMA,
        ],
        input_output_aliases=aliases,
        compiler_params=pltpu.CompilerParams(vmem_limit_bytes=40 * 2**20),
        cost_estimate=pl.CostEstimate(
            flops=250 * voxels, bytes_accessed=24 * voxels, transcendentals=0
        ),
        name=f"strip_{first}_{last}",
    )(*operands)


def shards(images, pairings):
    peers = lax.axis_size("img")
    slabs = lax.axis_size("space")
    me = lax.axis_index("img")
    slab = lax.axis_index("space")
    _, rows, height, width = images.shape
    partner_ids = lax.dynamic_slice_in_dim(pairings, me, 1, 1)[:, 0]
    up = [(i, i + 1) for i in range(slabs - 1)]
    down = [(i + 1, i) for i in range(slabs - 1)]

    if peers == 2:
        self_weight = jnp.sum((partner_ids == me).astype(jnp.float32))
        weights = [PAIRINGS - self_weight]

        def partners_of(piece):
            return lax.ppermute(piece, "img", [(0, 1), (1, 0)])

    else:
        self_weight = jnp.float32(0.0)
        weights = [jnp.float32(1.0)] * PAIRINGS

        def partners_of(piece):
            every = lax.all_gather(piece, "img", axis=0, tiled=True)
            return jnp.concatenate(
                [lax.dynamic_slice_in_dim(every, partner_ids[k], 1, 0) for k in range(PAIRINGS)]
            )

    scalars = jnp.stack(
        [(slab > 0).astype(jnp.float32), (slab < slabs - 1).astype(jnp.float32), self_weight, *weights]
    )

    own = images[0]
    edge = partners_of(jnp.concatenate([images[:, :HALO], images[:, rows - HALO :]], axis=1))
    cuts = list(zip(CUTS[:-1], CUTS[1:]))
    middles = [
        partners_of(images[:, HALO : rows - HALO, TILE * low : TILE * high]) for low, high in cuts
    ]
    own_halos = (
        lax.ppermute(own[rows - HALO :], "space", up),
        lax.ppermute(own[:HALO], "space", down),
    )
    far_halos = (
        lax.ppermute(edge[:, HALO:], "space", up),
        lax.ppermute(edge[:, :HALO], "space", down),
    )
    tiles = height // TILE
    ends = [high - 1 if high < tiles else tiles for _, high in cuts]
    first, outputs = 0, None
    for last in ends:
        outputs = run_strip(
            first, last, scalars, images, own_halos, edge, far_halos, middles, cuts, outputs
        )
        first = last
    return outputs


def solution(mesh):
    return jax.shard_map(
        shards,
        mesh=mesh,
        in_specs=(P("img", "space", None, None), P()),
        out_specs=(P("img", "space", None, None), P("img", None, "space", None, None)),
        check_vma=False,
    )
```
